128 devices in a mesh: seq: 16 (over x, z), head: 8 (over y, core).
Axes of the slice: x: 4, y: 4, z: 4, core: 2. Of those that a mesh axis runs over, the one named last changes fastest.
Arguments:
- tokens: bfloat16 [16384, 1024], P('seq'), may hold values from -6 to 6
- norm_gain: float32 [1024], replicated, may hold values from 0.5 to 1.5
- w_query: bfloat16 [1024, 1024], P(None, 'head'), may hold values from -0.1875 to 0.1875
- w_key: bfloat16 [1024, 1024], P(None, 'head'), may hold values from -0.1875 to 0.1875
- w_value: bfloat16 [1024, 2048], P(None, 'head'), may hold values from -0.1875 to 0.1875
- w_outgate: bfloat16 [1024, 2048], P(None, 'head'), may hold values from -0.1875 to 0.1875
- w_beta: float32 [1024, 8], P(None, 'head'), may hold values from -0.1875 to 0.1875
- w_decay: float32 [1024, 8], P(None, 'head'), may hold values from -0.1875 to 0.1875
- conv_query: float32 [4, 1024], P(None, 'head'), may hold values from -3 to 3
- conv_key: float32 [4, 1024], P(None, 'head'), may hold values from -3 to 3
- conv_value: float32 [4, 2048], P(None, 'head'), may hold values from -3 to 3
- decay_log: float32 [8], P('head'), may hold values from -7 to -2
- dt_bias: float32 [8], P('head'), may hold values from -1 to 1
- out_gain: float32 [256], replicated, may hold values from 0.5 to 1.5
- w_out: bfloat16 [2048, 1024], P('head'), may hold values from -0.1875 to 0.1875
- ffn_gain: float32 [1024], replicated, may hold values from 0.5 to 1.5
- w_gate: bfloat16 [1024, 2816], P(None, 'head'), may hold values from -0.1875 to 0.1875
- w_up: bfloat16 [1024, 2816], P(None, 'head'), may hold values from -0.1875 to 0.1875
- w_down: bfloat16 [2816, 1024], P('head'), may hold values from -0.21875 to 0.21875
- cotangent: bfloat16 [16384, 1024], P('seq'), may hold values from -6 to 6
Outputs:
- block_out: bfloat16 [16384, 1024], P('seq')
- grad_tokens: float32 [16384, 1024], P('seq')
- grad_norm_gain: float32 [1024], replicated
- grad_w_query: float32 [1024, 1024], P(None, 'head')
- grad_w_key: float32 [1024, 1024], P(None, 'head')
- grad_w_value: float32 [1024, 2048], P(None, 'head')
- grad_w_outgate: float32 [1024, 2048], P(None, 'head')
- grad_w_beta: float32 [1024, 8], P(None, 'head')
- grad_w_decay: float32 [1024, 8], P(None, 'head')
- grad_conv_query: float32 [4, 1024], P(None, 'head')
- grad_conv_key: float32 [4, 1024], P(None, 'head')
- grad_conv_value: float32 [4, 2048], P(None, 'head')
- grad_decay_log: float32 [8], P('head')
- grad_dt_bias: float32 [8], P('head')
- grad_out_gain: float32 [256], replicated
- grad_w_out: float32 [2048, 1024], P('head')
- grad_ffn_gain: float32 [1024], replicated
- grad_w_gate: float32 [1024, 2816], P(None, 'head')
- grad_w_up: float32 [1024, 2816], P(None, 'head')
- grad_w_down: float32 [2816, 1024], P('head')
The draws below stay inside these ranges and needn't reach their ends.
All inputs are finite; a program needn't handle non-finite values.
Results may differ from the reference program's by a relative error of at most 0.03.
The reference program's roundings to bfloat16 on the way (of `normed`, `gated` and `hidden`) count: a program that leaves them out, or rounds other values in their place, can miss the bound.
Values may be sent and summed in bfloat16 or wider, within the bound.
No kernel may reach another device: no remote copies, remote signals or barrier semaphores. Data moves between devices by JAX's collectives and lax.ppermute only.
A program may use at most 192 MiB of HBM per device.

```python
import jax
import jax.numpy as jnp
from jax import lax

D = 1024
HEADS = 8
KEY_DIM = 128
VALUE_DIM = 256
FF = 2816
CONV = 4
GROUP = 64
LENGTH = 16384


def block_levels(key, extent, shards, smallest, high):
    level, own = 1.0, jax.random.fold_in(key, 6)
    for axis_at, parts in shards:
        draws = jnp.exp(jax.random.uniform(jax.random.fold_in(own, axis_at), (parts,), jnp.float32, smallest / len(shards), high / len(shards)))
        level = level * jnp.repeat(draws, extent[axis_at] // parts).reshape([-1 if axis == axis_at else 1 for axis in range(len(extent))])
    return level


def centred(own_key, extent, scale, bound, pieces=(), dtype=jnp.bfloat16):
    level = block_levels(own_key, extent, pieces, -0.22, 0.18) if pieces else 1.0
    drawn = jax.random.normal(own_key, extent, jnp.float32) * scale * level
    return jnp.minimum(jnp.maximum(drawn, -bound), bound).astype(dtype)


def setup_inputs(seed: int = 0) -> dict:
    splits = jax.random.split(jax.random.key(seed), 21)
    return {
        "tokens": centred(splits[0], (LENGTH, D), 1.0, 6.0, ((0, 16),)),
        "norm_gain": jnp.clip(1.0 + 0.1 * jax.random.normal(splits[1], (D,), jnp.float32), 0.5, 1.5),
        "w_query": centred(splits[2], (D, HEADS * KEY_DIM), D ** -0.5, 0.1875, ((1, 8),)),
        "w_key": centred(splits[3], (D, HEADS * KEY_DIM), D ** -0.5, 0.1875, ((1, 8),)),
        "w_value": centred(splits[4], (D, HEADS * VALUE_DIM), D ** -0.5, 0.1875, ((1, 8),)),
        "w_outgate": centred(splits[5], (D, HEADS * VALUE_DIM), D ** -0.5, 0.1875, ((1, 8),)),
        "w_beta": centred(splits[6], (D, HEADS), D ** -0.5, 0.1875, ((1, 8),), jnp.float32),
        "w_decay": centred(splits[7], (D, HEADS), D ** -0.5, 0.1875, ((1, 8),), jnp.float32),
        "conv_query": centred(splits[8], (CONV, HEADS * KEY_DIM), CONV ** -0.5, 3.0, ((1, 8),), jnp.float32),
        "conv_key": centred(splits[9], (CONV, HEADS * KEY_DIM), CONV ** -0.5, 3.0, ((1, 8),), jnp.float32),
        "conv_value": centred(splits[10], (CONV, HEADS * VALUE_DIM), CONV ** -0.5, 3.0, ((1, 8),), jnp.float32),
        "decay_log": jnp.clip(-7.0 + 5.0 * jax.random.uniform(splits[11], (HEADS,), jnp.float32) ** block_levels(splits[11], (HEADS,), ((0, 8),), -0.2, 0.2), -7.0, -2.0),
        "dt_bias": jnp.clip(jax.random.uniform(splits[12], (HEADS,), jnp.float32, -1.0, 1.0) * block_levels(splits[12], (HEADS,), ((0, 8),), -0.4, 0.0), -1.0, 1.0),
        "out_gain": jnp.clip(1.0 + 0.1 * jax.random.normal(splits[13], (VALUE_DIM,), jnp.float32), 0.5, 1.5),
        "w_out": centred(splits[14], (HEADS * VALUE_DIM, D), (HEADS * VALUE_DIM // 2) ** -0.5, 0.1875, ((0, 8),)),
        "ffn_gain": jnp.clip(1.0 + 0.1 * jax.random.normal(splits[15], (D,), jnp.float32), 0.5, 1.5),
        "w_gate": centred(splits[16], (D, FF), D ** -0.5, 0.1875, ((1, 8),)),
        "w_up": centred(splits[17], (D, FF), D ** -0.5, 0.1875, ((1, 8),)),
        "w_down": centred(splits[18], (FF, D), (FF // 4) ** -0.5, 0.21875, ((0, 8),)),
        "cotangent": centred(splits[19], (LENGTH, D), 1.0, 6.0, ((0, 16),)),
    }


@jax.custom_vjp
def low(v):
    return lax.optimization_barrier(v.astype(jnp.bfloat16)).astype(jnp.float32)

@jax.custom_vjp
def low_back(v):
    return v

def low_keep(v):
    return (low(v), None)

def low_pass(kept, grad):
    return (grad,)

def back_keep(v):
    return (v, None)

def back_low(kept, grad):
    return (low(grad),)
low.defvjp(low_keep, low_pass)
low_back.defvjp(back_keep, back_low)
HIGH = lax.Precision.HIGHEST

def matmul(left, right):
    return jnp.dot(left, right, precision=HIGH)

def rms_norm(value, gain):
    return value * lax.rsqrt(lax.optimization_barrier(jnp.mean(value * value, -1, keepdims=True)) + 1e-05) * gain

def causal_conv(proj, taps):
    width = taps.shape[0]
    count = proj.shape[0]
    padded = jnp.pad(proj, ((width - 1, 0), (0, 0)))
    total = taps[0] * padded[0:count]
    for j in range(1, width):
        total = total + taps[j] * padded[j:j + count]
    return total

def unit_rows(value):
    return value * lax.rsqrt(lax.optimization_barrier(jnp.sum(value * value, -1, keepdims=True)) + 1e-06)

def recurrence(query, keys, values, beta, logdecay):
    count = query.shape[0]
    blocks = count // GROUP

    def split(a):
        return a.reshape((blocks, GROUP) + a.shape[1:])

    @jax.checkpoint
    def block_run(state, block):

        def token_step(state, item):
            qt, kt, vt, bt, gt = item
            state = jnp.exp(gt)[:, None, None] * state
            guess = jnp.einsum('hvk,hk->hv', state, kt, precision=HIGH)
            state = state + bt[:, None, None] * jnp.einsum('hv,hk->hvk', vt - guess, kt, precision=HIGH)
            return (state, jnp.einsum('hvk,hk->hv', state, qt, precision=HIGH))
        return lax.scan(token_step, state, block)
    start = jnp.zeros((HEADS, VALUE_DIM, KEY_DIM), jnp.float32)
    final, outs = lax.scan(block_run, start, (split(query), split(keys), split(values), split(beta), split(logdecay)))
    return outs.reshape(count, HEADS, VALUE_DIM)

def forward(x, norm_gain, w_query, w_key, w_value, w_outgate, w_beta, w_decay, conv_query, conv_key, conv_value, decay_log, dt_bias, out_gain, w_out, ffn_gain, w_gate, w_up, w_down):
    count = x.shape[0]
    normed = low(rms_norm(x, norm_gain))
    qp = low_back(low(matmul(normed, w_query)))
    kp = low_back(low(matmul(normed, w_key)))
    vp = low_back(low(matmul(normed, w_value)))
    gp = low_back(matmul(normed, w_outgate))
    bp = low_back(matmul(normed, w_beta))
    ap = low_back(matmul(normed, w_decay))
    query = unit_rows(jax.nn.silu(causal_conv(qp, conv_query)).reshape(count, HEADS, KEY_DIM)) * KEY_DIM ** (-0.5)
    keys = unit_rows(jax.nn.silu(causal_conv(kp, conv_key)).reshape(count, HEADS, KEY_DIM))
    values = jax.nn.silu(causal_conv(vp, conv_value)).reshape(count, HEADS, VALUE_DIM)
    beta = jax.nn.sigmoid(bp)
    logdecay = -jnp.exp(decay_log) * jax.nn.softplus(ap + dt_bias)
    mixed = recurrence(query, keys, values, beta, logdecay)
    gated = rms_norm(mixed, out_gain) * jax.nn.silu(gp.reshape(count, HEADS, VALUE_DIM))
    gated = low(gated.reshape(count, HEADS * VALUE_DIM))
    mid = x + low_back(matmul(gated, w_out))
    normed2 = low(rms_norm(mid, ffn_gain))
    gate = low_back(matmul(normed2, w_gate))
    upper = low_back(matmul(normed2, w_up))
    hidden = low(jax.nn.silu(gate) * upper)
    return mid + low_back(matmul(hidden, w_down))

def reference(tokens, norm_gain, w_query, w_key, w_value, w_outgate, w_beta, w_decay, conv_query, conv_key, conv_value, decay_log, dt_bias, out_gain, w_out, ffn_gain, w_gate, w_up, w_down, cotangent):
    inputs = (tokens, norm_gain, w_query, w_key, w_value, w_outgate, w_beta, w_decay, conv_query, conv_key, conv_value, decay_log, dt_bias, out_gain, w_out, ffn_gain, w_gate, w_up, w_down)
    floats = tuple((a.astype(jnp.float32) for a in inputs))
    result, pullback = jax.vjp(forward, *floats)
    grads = pullback(cotangent.astype(jnp.float32))
    return (result.astype(jnp.bfloat16), grads[0], grads[1], grads[2], grads[3], grads[4], grads[5], grads[6], grads[7], grads[8], grads[9], grads[10], grads[11], grads[12], grads[13], grads[14], grads[15], grads[16], grads[17], grads[18])
```

```python
from functools import partial

import jax
import jax.numpy as jnp
from jax import lax
from jax.experimental import pallas as pl
from jax.experimental.pallas import tpu as pltpu
from jax.sharding import PartitionSpec as P

C = 128
KD = 128
VD = 256
XD = VD + KD
NZ = 4
NX = 4
NY = 4
CORES = 2
HALF = 512
F32 = jnp.float32
BF = jnp.bfloat16
MA = F32
MS = F32
MH = BF
MT = BF
MC = BF
ML = BF
VMEM = pl.BlockSpec(memory_space=pltpu.VMEM)
SMEM = pl.BlockSpec(memory_space=pltpu.SMEM)


def split2(a):
    hi = a.astype(BF)
    return hi, (a - hi.astype(F32)).astype(BF)


def fdot(a, b, dims):
    a_parts = split2(a) if a.dtype == F32 else (a,)
    b_parts = split2(b) if b.dtype == F32 else (b,)
    total = None
    for i, x in enumerate(a_parts):
        for j, y in enumerate(b_parts):
            if i + j < 2:
                part = lax.dot_general(x, y, dims, preferred_element_type=F32)
                total = part if total is None else total + part
    return total


def nn(a, b):
    return fdot(a, b, (((1,), (0,)), ((), ())))


def nt(a, b):
    return fdot(a, b, (((1,), (1,)), ((), ())))


def tn(a, b):
    return fdot(a, b, (((0,), (0,)), ((), ())))


def sds(shape, dtype):
    return jax.ShapeDtypeStruct(shape, dtype)


def call(kernel, outs, args, scalars=0, scratch=()):
    return pl.pallas_call(
        kernel,
        out_shape=outs,
        in_specs=[SMEM] * scalars + [VMEM] * (len(args) - scalars),
        out_specs=jax.tree.map(lambda _: VMEM, outs),
        scratch_shapes=scratch,
        compiler_params=pltpu.CompilerParams(vmem_limit_bytes=56 * 1024 * 1024),
        cost_estimate=pl.CostEstimate(flops=1024, bytes_accessed=1024, transcendentals=0),
    )(*args)


def rows_of(c, size=C):
    return pl.ds(pl.multiple_of(c * size, size), size)


def square_iota():
    t = lax.broadcasted_iota(jnp.int32, (C, C), 0)
    s = lax.broadcasted_iota(jnp.int32, (C, C), 1)
    return t, s


def unit_lower_inverses(lowers, t, s):
    eye = jnp.where(t == s, 1.0, 0.0)
    apart = t ^ s
    xs = [eye - jnp.where(apart == 1, a, 0.0) for a in lowers]
    width = 2
    while width < C:
        inside = (apart >= width) & (apart < 2 * width)
        offs = [jnp.where(inside, a, 0.0).astype(BF) for a in lowers]
        xb = [x.astype(BF) for x in xs]
        ys = [nn(x, o).astype(BF) for x, o in zip(xb, offs)]
        xs = [x - nn(y, b) for x, y, b in zip(xs, ys, xb)]
        width *= 2
    xb = [x.astype(BF) for x in xs]
    parts = [split2(a) for a in lowers]
    rest = [
        (eye - b.astype(F32) - (nn(hi, b) + nn(lo, b))).astype(BF) for (hi, lo), b in zip(parts, xb)
    ]
    return [b.astype(F32) + nn(b, r) for b, r in zip(xb, rest)]


def activate(z):
    sig = jax.nn.sigmoid(z)
    act = z * sig
    aq, ak, av = act[:, :KD], act[:, KD : 2 * KD], act[:, 2 * KD :]
    rq = lax.rsqrt(jnp.sum(aq * aq, -1, keepdims=True) + 1e-06)
    rk = lax.rsqrt(jnp.sum(ak * ak, -1, keepdims=True) + 1e-06)
    return sig, aq * rq, ak * rk, av, rq, rk


def forward_local_kernel(
    tok, edge, gain, wq, wk, wv, wg, ws, taps, dl, dtb,
    normed, proj, gp, zs, small, uw_o, tinv_o, p_o, ag_o, qe_o, oloc_o, mp_o, x_o, total_o,
    nu_s, sw,
):
    w = ws[...]
    hi = w.astype(BF).astype(F32)
    mid = (w - hi).astype(BF).astype(F32)
    sw[...] = jnp.concatenate([hi, mid, w - hi - mid], 0).astype(BF)
    size = 256

    def project(x):
        n = x * lax.rsqrt(jnp.mean(x * x, -1, keepdims=True) + 1e-05) * gain[...]
        return n.astype(BF)

    ne = project(edge[...].astype(F32))
    proj[0:16, 0:KD] = nn(ne, wq[...]).astype(BF)
    proj[0:16, KD : 2 * KD] = nn(ne, wk[...]).astype(BF)
    proj[0:16, 2 * KD :] = nn(ne, wv[...]).astype(BF)

    def project_rows(i, _):
        rows = rows_of(i, size)
        n = project(tok[rows, :].astype(F32))
        normed[rows, :] = n
        put = pl.ds(pl.multiple_of(i * size + 16, 16), size)
        proj[put, 0:KD] = nn(n, wq[...]).astype(BF)
        proj[put, KD : 2 * KD] = nn(n, wk[...]).astype(BF)
        proj[put, 2 * KD :] = nn(n, wv[...]).astype(BF)
        gp[rows, :] = nn(n, wg[...])
        d = nt(n, sw[...])
        bp = d[:, 0:1] + d[:, 8:9] + d[:, 16:17]
        ap = d[:, 1:2] + d[:, 9:10] + d[:, 17:18] + dtb[...]
        rate = -jnp.exp(dl[...])
        lane = lax.broadcasted_iota(jnp.int32, (size, 8), 1)
        beta = jax.nn.sigmoid(bp)
        slope = rate * jax.nn.sigmoid(ap)
        logdecay = rate * (jnp.maximum(ap, 0.0) + jnp.log(1.0 + jnp.exp(-jnp.abs(ap))))
        small[rows, :] = jnp.where(
            lane == 0, beta, jnp.where(lane == 1, slope, jnp.where(lane == 2, logdecay, 0.0))
        )
        return 0

    lax.fori_loop(0, tok.shape[0] // size, project_rows, 0)

    t, s = square_iota()
    eye = t == s
    group = 4

    def chunks(g, _):
        cs = [g * group + i for i in range(group)]
        qs, ks, lowers, rhs, carried = [], [], [], [], []
        ps, qgs, egs = [], [], []
        for c in cs:
            rows = rows_of(c)
            window = proj[pl.ds(pl.multiple_of(c * C, C), C + 16), :].astype(F32)
            z = taps[0:1, :] * window[13 : 13 + C]
            for j in range(1, 4):
                z = z + taps[j : j + 1, :] * window[13 + j : 13 + j + C]
            zs[rows, :] = z
            _, qn, k, v, _, _ = activate(z)
            q = qn * KD ** (-0.5)
            sm = small[rows, :]
            beta, ld = sm[:, 0:1], sm[:, 2:3]
            grow = jnp.sum(jnp.where(t <= s, ld, 0.0), 0, keepdims=True)
            gcol = jnp.sum(jnp.where(eye, grow, 0.0), 1, keepdims=True)
            last = grow[:, C - 1 : C]
            decay = jnp.where(t >= s, jnp.exp(jnp.where(t >= s, gcol - grow, 0.0)), 0.0)
            lane = lax.broadcasted_iota(jnp.int32, (C, 8), 1)
            small[rows, :] = jnp.where(lane == 3, gcol, sm)
            kb, qb = k.astype(MA), q.astype(MA)
            both = nt(jnp.concatenate([kb, qb], 0), kb)
            ag = jnp.where(t > s, decay * both[:C], 0.0)
            p = decay * both[C:]
            ag_o[rows, :] = ag.astype(MA)
            pb = p.astype(MA)
            p_o[rows, :] = pb
            ps.append(pb)
            lowers.append(beta * ag)
            eg = jnp.exp(gcol)
            rhs.append(jnp.concatenate([beta * v, (beta * eg) * k], 1).astype(MA))
            carried.append((jnp.exp(last - gcol) * k).astype(MA))
            qgs.append(eg * q)
            egs.append(jnp.exp(last))
        inverses = [x.astype(MA) for x in unit_lower_inverses(lowers, t, s)]
        uws = [nn(x, r).astype(MA) for x, r in zip(inverses, rhs)]
        nus = [tn(k, uw) for k, uw in zip(carried, uws)]
        puws = [nn(p, uw) for p, uw in zip(ps, uws)]
        for i, c in enumerate(cs):
            rows = rows_of(c)
            tinv_o[rows, :] = inverses[i]
            uw_o[rows, :] = uws[i]
            qe_o[rows, :] = (qgs[i] - puws[i][:, VD:]).astype(MA)
            oloc_o[rows, :] = puws[i][:, :VD]
            nu_s[rows, :] = nus[i][:, :VD]
            mp_o[rows, :] = nus[i][:, VD:].astype(MS)
        return 0

    count = tok.shape[0] // C
    lax.fori_loop(0, count // group, chunks, 0)

    state = jnp.concatenate([jnp.zeros((KD, VD), F32), jnp.where(eye, 1.0, 0.0)], 1)
    for c in range(count):
        rows = slice(c * C, (c + 1) * C)
        sb = state.astype(MS)
        x_o[rows, :] = sb
        eg = jnp.exp(small[(c + 1) * C - 1 : (c + 1) * C, 3:4])
        new = eg * state - nn(mp_o[rows, :], sb)
        state = jnp.concatenate([new[:, :VD] + nu_s[rows, :], new[:, VD:]], 1)
    total_o[...] = state.astype(ML)


def ordered(own, others, place, count):
    scratch, refs = others
    scratch[place] = own[...]
    for k, ref in enumerate(refs, 1):
        scratch[lax.rem(place + count - k, count)] = ref[...]


def apply_to(m, y):
    return nn(m, y)


def apply_transposed(m, y):
    return tn(m, y)


def start_state():
    t, s = square_iota()
    return jnp.concatenate([jnp.zeros((KD, VD), F32), jnp.where(t == s, 1.0, 0.0)], 1)


def add_left(y, left):
    return jnp.concatenate([y[:, :VD] + left.astype(F32), y[:, VD:]], 1)


def combine_kernel(place, own, r1, r2, r3, total, before, slots):
    z = place[1]
    ordered(own, (slots, (r1, r2, r3)), z, NZ)
    y = start_state()
    seen = y
    for i in range(NZ):
        seen = jnp.where(i == z, y, seen)
        y = add_left(apply_to(slots[i, :, VD:], y), slots[i, :, :VD])
    total[...] = y.astype(ML)
    before[...] = seen


def mix_out_kernel(
    place, own, r1, r2, r3, before, x_i, qe, oloc, uw, gp, gain, wout,
    hs, o, delta, gated, keep, send, slots,
):
    x, y_at, core = place[0], place[2], place[3]
    ordered(own, (slots, (r1, r2, r3)), x, NX)
    h = jnp.zeros((KD, VD), F32)
    for i in range(NX - 1):
        h = jnp.where(i < x, apply_to(slots[i, :, VD:], h) + slots[i, :, :VD].astype(F32), h)
    b = before[...]
    h0 = nn(b[:, VD:].astype(MS), h.astype(MS)) + b[:, :VD]
    h0b = h0.astype(MS)

    def mix_rows(i, base, out_ref):
        for j in range(2):
            rows = pl.ds(pl.multiple_of(base + i * 2 * C + j * C, C), C)
            xc = x_i[rows, :]
            hc = (nn(xc[:, VD:], h0b) + xc[:, :VD].astype(F32)).astype(MH)
            hs[rows, :] = hc
            u = uw[rows, :]
            both = nn(jnp.concatenate([qe[rows, :], u[:, VD:]], 0), hc)
            out = both[:C] + oloc[rows, :]
            delta[rows, :] = (u[:, :VD].astype(F32) - both[C:]).astype(MH)
            o[rows, :] = out
            g = gp[rows, :]
            y = out * lax.rsqrt(jnp.mean(out * out, -1, keepdims=True) + 1e-05)
            gated[rows, :] = (y * gain[...] * (g * jax.nn.sigmoid(g))).astype(BF)
        rows = pl.ds(pl.multiple_of(base + i * 2 * C, 2 * C), 2 * C)
        put_slots(out_ref, nn(gated[rows, :], wout[...]).astype(BF), 2 * i, y_at)

    halves(mix_rows, core, keep, send)


def halves(body, core, keep, send):
    for half, target in ((1 - core, send), (core, keep)):

        def step(i, _, half=half, target=target):
            body(i, half * HALF, target)
            return 0

        lax.fori_loop(0, HALF // (2 * C), step, 0)


def put_slots(target, pair, block, y_at):
    for j in range(2):
        slot = lax.rem(block + j - y_at + 2 * NY, NY)
        target[rows_of(slot), :] = pair[j * C : (j + 1) * C]


def arrived(body, place, blocks, keep, send):
    y_at, core = place[2], place[3]
    for half, source, target in ((core, blocks[:NY], keep), (1 - core, blocks[NY:], send)):
        for i in range(0, NY, 2):
            rows, slots = [], []
            for j in (i, i + 1):
                block = lax.rem(y_at - j + NY, NY)
                rows.append(pl.ds(pl.multiple_of(half * HALF + block * C, C), C))
                slots.append(slice((NY - j) % NY * C, ((NY - j) % NY + 1) * C))
            body(jnp.concatenate([source[i][...], source[i + 1][...]], 0), rows, target, slots)


def two(ref, rows):
    return jnp.concatenate([ref[rows[0], :], ref[rows[1], :]], 0)


def put_two(ref, rows, value):
    ref[rows[0], :] = value[:C]
    ref[rows[1], :] = value[C:]


def pair_sum_kernel(keep, got, p0, p1, p2, p3):
    p0[0:C, :] = keep[0:C, :].astype(F32) + got[0:C, :].astype(F32)
    for k, ref in ((1, p1), (2, p2), (3, p3)):
        rows = slice(k * C, (k + 1) * C)
        ref[0:C, :] = (keep[rows, :].astype(F32) + got[rows, :].astype(F32)).astype(BF)
    if keep.shape[0] > HALF:
        extra = keep[HALF:, :].astype(F32) + got[HALF:, :].astype(F32)
        p0[C:, :] = extra
        for ref in (p1, p2, p3):
            ref[C:, :] = extra.astype(BF)


def four(p0, r1, r2, r3):
    return p0[...] + (r1[...].astype(F32) + r2[...].astype(F32) + r3[...].astype(F32))


def mid_kernel(p0, r1, r2, r3, x, gain, mid_o, n_o):
    mid = x[...].astype(F32) + four(p0, r1, r2, r3)
    mid_o[...] = mid
    n = mid * lax.rsqrt(jnp.mean(mid * mid, -1, keepdims=True) + 1e-05) * gain[...]
    n_o[...] = n.astype(BF)


def block_out_kernel(p0, r1, r2, r3, mid, out):
    out[...] = (mid[...] + four(p0, r1, r2, r3)).astype(BF)


def dmid_kernel(p0, r1, r2, r3, mid, cot, gain, dmid, dmidb, dgain):
    dx, dg = rms_back(mid[...], four(p0, r1, r2, r3), gain[...])
    dm = cot[...].astype(F32) + dx
    dmid[...] = dm
    dmidb[...] = dm.astype(BF)
    dgain[...] = dg


def dx_kernel(p0, r1, r2, r3, x, dmid, gain, dtaps, dscal, gsmall, out, vec):
    total = four(p0, r1, r2, r3)
    dx, _ = rms_back(x[...].astype(F32), total[:C], gain[...])
    out[...] = (dmid[...] + dx).astype(BF)
    vec[0:3, :] = total[C : C + 3]
    for j in range(4):
        vec[3 + j // 2 : 4 + j // 2, (j % 2) * HALF : (j % 2 + 1) * HALF] = dtaps[j : j + 1, :]
    vec[5:7, :] = gsmall[0:2, :]
    vec[7:8, :] = jnp.concatenate([dscal[...], jnp.zeros((1, vec.shape[1] - 128), F32)], 1)


def assemble_kernel(place, *refs):
    out = refs[-1]

    def body(value, rows, target, slots):
        put_two(out, rows, value.astype(out.dtype))

    arrived(body, place, refs[:-1], None, None)


def ring_places(place):
    return place[4], place[5]


def proj_grad_kernel(place, normed, dproj, own, s1, s2, s3):
    u, _ = ring_places(place)
    size = own.shape[0]
    for k, ref in enumerate((own, s1, s2, s3)):
        block = lax.rem(u + k, NZ)
        part = normed[:, pl.ds(pl.multiple_of(block * size, size), size)]
        ref[...] = tn(part, dproj[...]).astype(ref.dtype)


def pack_vector(vec):
    hi, lo = split2(vec)
    hi, lo = hi.astype(F32), lo.astype(F32)
    half = vec.shape[1] // 2
    return jnp.concatenate([hi[:, :half], hi[:, half:], lo[:, :half], lo[:, half:]], 0).astype(BF)


def unpack_vector(rows):
    rows = rows.astype(F32)
    both = rows[0:16] + rows[16:32]
    return jnp.concatenate([both[0:8], both[8:16]], 1)


def grad_pack_kernel(own, r1, r2, r3, vec, out):
    size = own.shape[0]
    out[0:size, :] = four(own, r1, r2, r3).astype(BF)
    out[size:, :] = pack_vector(vec[...])


def grad_join_kernel(place, m0, m1, m2, m3, out, slots):
    _, w = ring_places(place)
    ordered(m0, (slots, (m1, m2, m3)), w, NX)
    size = m0.shape[0] - 32
    total = sum(slots[i, 0:size, :].astype(F32) for i in range(NX))
    out[0:size, :] = total.astype(BF)
    out[size:, :] = pack_vector(sum(unpack_vector(slots[i, size:, :]) for i in range(NX)))


def grad_final_kernel(
    place, n0, n1, n2, n3, gq, gk, gv, gain, fgain, ogain, tq, tk, tv, gb, ga, scal, slots
):
    u, _ = ring_places(place)
    ordered(n0, (slots, (n1, n2, n3)), u, NZ)
    size = n0.shape[0] - 32
    for i in range(NZ):
        rows = slice(i * size, (i + 1) * size)
        value = slots[i, 0:size, :].astype(F32)
        gq[rows, :] = value[:, :KD]
        gk[rows, :] = value[:, KD : 2 * KD]
        gv[rows, :] = value[:, 2 * KD :]
    vec = sum(unpack_vector(slots[i, size:, :]) for i in range(NZ))
    gain[...] = vec[0:1]
    fgain[...] = vec[1:2]
    ogain[...] = vec[2:3, :VD]
    for j in range(4):
        tap = vec[3 + j // 2 : 4 + j // 2, (j % 2) * HALF : (j % 2 + 1) * HALF]
        tq[j : j + 1, :] = tap[:, :KD]
        tk[j : j + 1, :] = tap[:, KD : 2 * KD]
        tv[j : j + 1, :] = tap[:, 2 * KD :]
    gb[...] = vec[5:6]
    ga[...] = vec[6:7]
    scal[...] = vec[7:8, :128]


def hidden_grad_kernel(cot, wd, out):
    def step(i, _):
        rows = rows_of(i, 2 * C)
        out[rows, :] = nt(cot[rows, :], wd[...])
        return 0

    lax.fori_loop(0, out.shape[0] // (2 * C), step, 0)


def mlp_kernel(place, hidden, wd, keep, send):
    def rows_step(i, base, target):
        rows = pl.ds(pl.multiple_of(base + i * 2 * C, 2 * C), 2 * C)
        put_slots(target, nn(hidden[rows, :], wd[...]).astype(BF), 2 * i, place[2])

    halves(rows_step, place[3], keep, send)


def ffn_kernel(
    place, b0, b1, b2, b3, b4, b5, b6, b7, wg, wu, dh, normed2, hidden, dgate, dup, keep, send
):
    def body(n, rows, target, slots):
        put_two(normed2, rows, n)
        gate = nt(n, wg[...])
        up = nt(n, wu[...])
        sig = jax.nn.sigmoid(gate)
        act = gate * sig
        put_two(hidden, rows, (act * up).astype(BF))
        d = two(dh, rows)
        du = (d * act).astype(BF)
        dg = (d * up * (sig + act * (1.0 - sig))).astype(BF)
        put_two(dgate, rows, dg)
        put_two(dup, rows, du)
        put_two(target, slots, (nn(dg, wg[...]) + nn(du, wu[...])).astype(BF))

    arrived(body, place, (b0, b1, b2, b3, b4, b5, b6, b7), keep, send)


def rms_back(x, dn, gain):
    r = lax.rsqrt(jnp.mean(x * x, -1, keepdims=True) + 1e-05)
    xn = x * r
    dg = dn * gain
    dx = r * (dg - xn * jnp.mean(dg * xn, -1, keepdims=True))
    return dx, jnp.sum(dn * xn, 0, keepdims=True)


def mix_back_kernel(
    place, b0, b1, b2, b3, b4, b5, b6, b7, wout, gp, o, ogain, qe, mp, small,
    dmidb, do, dgp, dogain, y_o, b_o, qd_s,
):
    dogain[...] = jnp.zeros_like(dogain)

    def body(dmb, rows, target, slots):
        put_two(dmidb, rows, dmb)
        dgated = nt(dmb, wout[...])
        out = two(o, rows)
        g = two(gp, rows)
        ro = lax.rsqrt(jnp.mean(out * out, -1, keepdims=True) + 1e-05)
        y = out * ro
        sig = jax.nn.sigmoid(g)
        act = g * sig
        dy = dgated * ogain[...] * act
        put_two(dgp, rows, (dgated * y * ogain[...] * (sig + act * (1.0 - sig))).astype(BF))
        dogain[...] += jnp.sum(dgated * y * act, 0, keepdims=True)
        dob = (ro * (dy - y * jnp.mean(dy * y, -1, keepdims=True))).astype(MT)
        put_two(do, rows, dob)
        for j in range(2):
            qd_s[rows[j], :] = tn(qe[rows[j], :], dob[j * C : (j + 1) * C])

    arrived(body, place, (b0, b1, b2, b3, b4, b5, b6, b7), None, None)
    state = start_state()
    for c in reversed(range(gp.shape[0] // C)):
        rows = slice(c * C, (c + 1) * C)
        sb = state.astype(MT)
        y_o[rows, :] = sb
        eg = jnp.exp(small[(c + 1) * C - 1 : (c + 1) * C, 3:4])
        state = add_left(eg * state - tn(mp[rows, :], sb), qd_s[rows, :])
    b_o[...] = state[:, :VD].astype(ML)


def combine_back_kernel(place, own, r1, r2, r3, f0, f1, f2, f3, total, after, slots, fslots):
    z = place[1]
    ordered(own, (slots, (r1, r2, r3)), z, NZ)
    ordered(f0, (fslots, (f1, f2, f3)), z, NZ)
    y = start_state()
    seen = y
    for i in reversed(range(NZ)):
        seen = jnp.where(i == z, y, seen)
        y = add_left(apply_transposed(fslots[i, :, VD:], y), slots[i])
    total[...] = y[:, :VD].astype(ML)
    after[...] = seen


def chunk_back_kernel(
    place, own, r1, r2, r3, f0, f1, f2, f3, after, y_i, hs, delta, do, tinv, pm, agm, zs, small, proj,
    dz, dsmall, dtaps, dscal, slots, fslots,
):
    x = place[0]
    ordered(own, (slots, (r1, r2, r3)), x, NX)
    ordered(f0, (fslots, (f1, f2, f3)), x, NX)
    e = jnp.zeros((KD, VD), F32)
    for i in reversed(range(1, NX)):
        e = jnp.where(i > x, apply_transposed(fslots[i, :, VD:], e) + slots[i].astype(F32), e)
    a = after[...]
    e0 = (nn(a[:, VD:].astype(MT), e.astype(MT)) + a[:, :VD]).astype(MT)

    t, s = square_iota()
    eye = t == s
    dtaps[...] = jnp.zeros_like(dtaps)
    dscal[...] = jnp.zeros_like(dscal)
    group = 2

    def chunk(c):
        rows = rows_of(c)
        z = zs[rows, :]
        sig, qn, k, v, rq, rk = activate(z)
        q = qn * KD ** (-0.5)
        kb, qb = k.astype(MC), q.astype(MC)
        sm = small[rows, :]
        beta, slope, ld, gcol = sm[:, 0:1], sm[:, 1:2], sm[:, 2:3], sm[:, 3:4]
        grow = jnp.sum(jnp.where(eye, gcol, 0.0), 0, keepdims=True)
        last = grow[:, C - 1 : C]
        decay = jnp.where(t >= s, jnp.exp(jnp.where(t >= s, gcol - grow, 0.0)), 0.0)
        eg = jnp.exp(gcol)
        back = jnp.exp(last - gcol)
        yc = y_i[rows, :]
        h = hs[rows, :]
        dlt = delta[rows, :]
        dob = do[rows, :]
        d = nn(yc[:, VD:], e0) + yc[:, :VD].astype(F32)
        db = d.astype(MT)
        kc = (back * k).astype(MC)
        ddelta = (tn(pm[rows, :], dob) + nn(kc, db)).astype(MC)
        ru = tn(tinv[rows, :], ddelta)
        rub = ru.astype(MC)
        four = nt(jnp.concatenate([rub, dob], 0), jnp.concatenate([dlt, h], 0))
        da = jnp.where(t > s, -four[:C, :C], 0.0)
        dp = jnp.where(t >= s, four[C:, :C], 0.0)
        rw = -four[:C, C:]
        dqg = four[C:, C:]
        dkc = nt(dlt, db)
        ag = agm[rows, :].astype(F32)
        p = pm[rows, :].astype(F32)
        dag = da * ag
        dpd = (dp * decay).astype(MC)
        dad = (da * (beta * decay)).astype(MC)
        first = nn(jnp.concatenate([dpd, dad], 0), kb)
        second = tn(jnp.concatenate([dad, dpd], 0), jnp.concatenate([kb, qb], 0))
        dq = eg * dqg + first[:C]
        dk = (beta * eg) * rw + back * dkc + first[C:] + second
        dv = beta * ru
        rwk = eg * jnp.sum(rw * k, 1, keepdims=True)
        dbeta = jnp.sum(ru * v, 1, keepdims=True) + rwk + jnp.sum(dag, 1, keepdims=True)
        zz = beta * dag + dp * p
        kk = back * jnp.sum(dkc * k, 1, keepdims=True)
        dg = beta * rwk + eg * jnp.sum(dqg * q, 1, keepdims=True) - kk + jnp.sum(zz, 1, keepdims=True)
        ends = jnp.sum(kk, 0, keepdims=True) + jnp.exp(last) * jnp.sum(
            jnp.sum(d * h.astype(F32), 1, keepdims=True), 0, keepdims=True
        )
        grow_d = jnp.sum(jnp.where(eye, dg, 0.0), 0, keepdims=True) - jnp.sum(zz, 0, keepdims=True)
        dld = jnp.sum(jnp.where(s >= t, grow_d, 0.0), 1, keepdims=True) + ends
        dap = dld * slope
        dbp = dbeta * beta * (1.0 - beta)
        lane = lax.broadcasted_iota(jnp.int32, (C, 8), 1)
        dsmall[rows, :] = jnp.where(lane == 0, dbp, jnp.where(lane == 1, dap, 0.0))
        wide = lax.broadcasted_iota(jnp.int32, (C, 128), 1)
        dscal[...] += jnp.sum(
            jnp.where(wide == 0, dld * ld, jnp.where(wide == 1, dap, 0.0)), 0, keepdims=True
        )
        dqs = (KD ** (-0.5)) * rq * (dq - qn * jnp.sum(qn * dq, -1, keepdims=True))
        dks = rk * (dk - k * jnp.sum(k * dk, -1, keepdims=True))
        dact = jnp.concatenate([dqs, dks, dv], 1)
        dzc = dact * (sig * (1.0 + z * (1.0 - sig)))
        dz[rows, :] = dzc
        window = proj[pl.ds(pl.multiple_of(c * C, C), C + 16), :].astype(F32)
        for j in range(4):
            dtaps[j : j + 1, :] += jnp.sum(dzc * window[13 + j : 13 + j + C], 0, keepdims=True)

    def chunks(g, _):
        for i in range(group):
            chunk(g * group + i)
        return 0

    lax.fori_loop(0, hs.shape[0] // (C * group), chunks, 0)


def project_back_kernel(
    place, dz, nxt, taps, dgp, dsmall, wq, wk, wv, wg, ws, tok, gain, dfgain, dogain,
    dproj, dsb, keep, send, pad, dgain,
):
    count = dz.shape[0]
    pad[0:count, :] = dz[...]
    pad[count : count + 8, :] = nxt[...]
    dgain[...] = jnp.zeros_like(dgain)
    size = 2 * C

    def body(i, base, target):
        at = base + i * size
        rows = pl.ds(pl.multiple_of(at, size), size)
        window = pad[pl.ds(pl.multiple_of(at, size), size + 8), :]
        total = taps[3:4, :] * window[0:size]
        for j in range(3):
            total = total + taps[j : j + 1, :] * window[3 - j : 3 - j + size]
        tb = total.astype(BF)
        dproj[rows, :] = tb
        sb = dsmall[rows, :].astype(BF)
        dsb[rows, :] = sb
        dn = (
            nt(tb[:, :KD], wq[...])
            + nt(tb[:, KD : 2 * KD], wk[...])
            + nt(tb[:, 2 * KD :], wv[...])
            + nt(dgp[rows, :], wg[...])
            + nn(sb, ws[...].astype(BF))
        )
        x = tok[rows, :].astype(F32)
        xn = x * lax.rsqrt(jnp.mean(x * x, -1, keepdims=True) + 1e-05)
        dgain[...] += jnp.sum(dn * xn, 0, keepdims=True)
        put_slots(target, dn.astype(BF), 2 * i, place[2])

    halves(body, place[3], keep, send)
    wide = jnp.concatenate([dogain[...], jnp.zeros((1, tok.shape[1] - VD), F32)], 1)
    vec = jnp.concatenate([dgain[...], dfgain[...], wide, jnp.zeros((13, tok.shape[1]), F32)], 0)
    keep[HALF:, :] = vec.astype(BF)
    send[HALF:, :] = vec.astype(BF)


def around(value, axis_z, k):
    pairs = []
    for x in range(NX):
        for z in range(NZ):
            to = (x, (z + k) % NZ) if axis_z else ((x + k) % NX, z)
            pairs.append((x * NZ + z, to[0] * NZ + to[1]))
    return lax.ppermute(value, "seq", pairs)


def swap_core(value):
    count = lax.axis_size("head")
    return lax.ppermute(value, "head", [(h, h ^ 1) for h in range(count)])


def along_y(value, k):
    count = lax.axis_size("head")
    return lax.ppermute(value, "head", [(h, (h + CORES * k) % count) for h in range(count)])


def chip_sum(keep, send):
    rows, width = keep.shape
    extra = rows - HALF
    got = swap_core(send)
    return call(
        pair_sum_kernel,
        (sds((C + extra, width), F32),) + (sds((C + extra, width), BF),) * 3,
        (keep, got),
    )


def chip_parts(parts):
    return [parts[0]] + [along_y(p, k) for k, p in enumerate(parts[1:], 1)]


def scatter_sum(keep, send):
    return chip_parts(chip_sum(keep, send))


def gather_chips(shard):
    return [shard] + [along_y(shard, k) for k in range(1, NY)]


def gather_rows(shard):
    own = gather_chips(shard)
    return own + [swap_core(part) for part in own]


def seq_ring(value, first, k):
    heads = lax.axis_size("head")
    pairs = []
    for x in range(NX):
        for z in range(NZ):
            for h in range(heads):
                by_z = first == (h % CORES == 0)
                to = (x, (z + k) % NZ) if by_z else ((x + k) % NX, z)
                pairs.append(((x * NZ + z) * heads + h, (to[0] * NZ + to[1]) * heads + h))
    return lax.ppermute(value, ("seq", "head"), pairs)


def ring_all(value, first):
    return [value] + [seq_ring(value, first, k) for k in range(1, NZ)]


def ring_scatter(own, *parts, first):
    return [own] + [seq_ring(part, first, k) for k, part in enumerate(parts, 1)]


def weight_dot(left, right):
    return lax.dot_general(
        left, right, (((0,), (0,)), ((), ())), preferred_element_type=F32
    ).astype(BF)


def per_device(
    tokens, norm_gain, w_query, w_key, w_value, w_outgate, w_beta, w_decay, conv_query, conv_key,
    conv_value, decay_log, dt_bias, out_gain, w_out, ffn_gain, w_gate, w_up, w_down, cotangent,
):
    count, width = tokens.shape
    ff = w_gate.shape[1]
    seq = lax.axis_index("seq")
    head = lax.axis_index("head")
    y_at, core = head // CORES, lax.rem(head, CORES)
    x_at, z_at = seq // NZ, lax.rem(seq, NZ)
    rings = (jnp.where(core == 0, z_at, x_at), jnp.where(core == 0, x_at, z_at))
    place = jnp.stack([x_at, z_at, y_at, core, *rings]).astype(jnp.int32)
    mine = (core * NY + y_at) * C
    x_own = lax.dynamic_slice(tokens, (mine, 0), (C, width))
    cot_own = lax.dynamic_slice(cotangent, (mine, 0), (C, width))
    half = sds((HALF, width), BF)
    shard = sds((C, width), F32)
    shard_b = sds((C, width), BF)
    devices = lax.axis_size("seq")
    gain = norm_gain.reshape(1, width)
    fgain = ffn_gain.reshape(1, width)
    ogain = out_gain.reshape(1, VD)
    taps = jnp.concatenate([conv_query, conv_key, conv_value], 1)
    ws = jnp.concatenate(
        [w_beta.reshape(1, width), w_decay.reshape(1, width), jnp.zeros((6, width), F32)], 0
    )
    edge = lax.ppermute(tokens[-16:], "seq", [(i, i + 1) for i in range(devices - 1)])
    (dh,) = call(hidden_grad_kernel, (sds((count, ff), F32),), (cotangent, w_down))
    edge, dh = lax.optimization_barrier((edge, dh))

    sqa = sds((count, C), MA)
    sqs = sds((count, C), MS)
    (
        normed, proj, gp, zs, small, uw, tinv, pm, agm, qe, oloc, mp, xs, total,
    ) = call(
        forward_local_kernel,
        (
            sds((count, width), BF), sds((count + 16, 2 * KD + VD), BF), sds((count, VD), F32),
            sds((count, 2 * KD + VD), F32), sds((count, 8), F32), sds((count, XD), MA), sqa,
            sqa, sqa, sqa, sds((count, VD), F32), sqs, sds((count, XD), MS),
            sds((KD, XD), ML),
        ),
        (
            tokens, edge, gain, w_query, w_key, w_value, w_outgate, ws, taps,
            decay_log.reshape(1, 1), dt_bias.reshape(1, 1),
        ),
        scratch=[pltpu.VMEM((count, VD), F32), pltpu.VMEM((24, width), BF)],
    )

    ftz = [total] + [around(total, True, k) for k in range(1, NZ)]
    group, before = call(
        combine_kernel,
        (sds((KD, XD), ML), sds((KD, XD), F32)),
        (place, *ftz),
        scalars=1,
        scratch=[pltpu.VMEM((NZ, KD, XD), ML)],
    )
    ftx = [group] + [around(group, False, k) for k in range(1, NX)]
    hs, o, delta, gated, keep, send = call(
        mix_out_kernel,
        (
            sds((count, VD), MH), sds((count, VD), F32), sds((count, VD), MH),
            sds((count, VD), BF), half, half,
        ),
        (place, *ftx, before, xs, qe, oloc, uw, gp, ogain, w_out),
        scalars=1,
        scratch=[pltpu.VMEM((NX, KD, XD), ML)],
    )
    mid, n2 = call(
        mid_kernel, (shard, shard_b), (*scatter_sum(keep, send), x_own, fgain)
    )
    normed2, hidden, dgate, dup, keep, send = call(
        ffn_kernel,
        (
            sds((count, width), BF), sds((count, ff), BF), sds((count, ff), BF),
            sds((count, ff), BF), half, half,
        ),
        (place, *gather_rows(n2), w_gate.T, w_up.T, dh),
        scalars=1,
    )
    parts = scatter_sum(keep, send)
    mlp = call(mlp_kernel, (half, half), (place, hidden, w_down), scalars=1)
    parts, mlp = lax.optimization_barrier((parts, mlp))
    dmid, dmid_b, d_fgain = call(
        dmid_kernel, (shard, shard_b, sds((1, width), F32)), (*parts, mid, cot_own, fgain)
    )
    dm_rows = gather_rows(dmid_b)
    grads = (
        weight_dot(normed2, dgate), weight_dot(normed2, dup), weight_dot(hidden, cotangent)
    )
    mlp = chip_sum(*mlp)
    dm_rows, grads, mlp = lax.optimization_barrier((dm_rows, grads, mlp))
    mlp = chip_parts(mlp)
    dmidb, do, dgp, d_ogain, ys, b0 = call(
        mix_back_kernel,
        (
            sds((count, width), BF), sds((count, VD), MT), sds((count, VD), BF),
            sds((1, VD), F32), sds((count, XD), MT), sds((KD, VD), ML),
        ),
        (place, *dm_rows, w_out, gp, o, ogain, qe, mp, small),
        scalars=1,
        scratch=[pltpu.VMEM((count, VD), F32)],
    )
    g_out = weight_dot(gated, dmidb)
    g_outgate = weight_dot(normed, dgp)

    btz = [b0] + [around(b0, True, k) for k in range(1, NZ)]
    btz, mlp = lax.optimization_barrier((btz, mlp))
    bgroup, after = call(
        combine_back_kernel,
        (sds((KD, VD), ML), sds((KD, XD), F32)),
        (place, *btz, *ftz),
        scalars=1,
        scratch=[pltpu.VMEM((NZ, KD, VD), ML), pltpu.VMEM((NZ, KD, XD), ML)],
    )
    grads = (*grads, g_out, g_outgate)
    bgroup, grads = lax.optimization_barrier((bgroup, grads))
    summed = lax.psum(grads, "seq")
    btx = [bgroup] + [around(bgroup, False, k) for k in range(1, NX)]
    (bout,) = call(block_out_kernel, (shard_b,), (*mlp, mid))
    btx, bout = lax.optimization_barrier((btx, bout))
    dz, dsmall, dtaps, dscal = call(
        chunk_back_kernel,
        (
            sds((count, 2 * KD + VD), F32), sds((count, 8), F32), sds((4, 2 * KD + VD), F32),
            sds((1, 128), F32),
        ),
        (place, *btx, *ftx, after, ys, hs, delta, do, tinv, pm, agm, zs, small, proj),
        scalars=1,
        scratch=[pltpu.VMEM((NX, KD, VD), ML), pltpu.VMEM((NX, KD, XD), ML)],
    )
    bo = gather_chips(bout)
    dz, bo = lax.optimization_barrier((dz, bo))
    bo = bo + [swap_core(part) for part in bo]
    nxt = lax.ppermute(dz[:8], "seq", [(i + 1, i) for i in range(devices - 1)])
    (block_out,) = call(
        assemble_kernel, (sds((count, width), BF),), (place, *bo), scalars=1,
    )
    nxt, block_out = lax.optimization_barrier((nxt, block_out))
    dproj, dsb, keep, send = call(
        project_back_kernel,
        (sds((count, 2 * KD + VD), BF), sds((count, 8), BF)) + (sds((HALF + 16, width), BF),) * 2,
        (
            place, dz, nxt, taps, dgp, dsmall, w_query, w_key, w_value, w_outgate, ws, tokens,
            gain, d_fgain, d_ogain,
        ),
        scalars=1,
        scratch=[pltpu.VMEM((count + 8, 2 * KD + VD), F32), pltpu.VMEM((1, width), F32)],
    )
    parts = scatter_sum(keep, send)
    blocks = sds((width // NZ, 2 * KD + VD), F32)
    sent = call(
        proj_grad_kernel,
        (blocks,) + (sds(blocks.shape, BF),) * 3,
        (place, normed, dproj),
        scalars=1,
    )
    sent, parts = lax.optimization_barrier((sent, parts))
    g_small = lax.dot_general(dsb, normed, (((0,), (0,)), ((), ())), preferred_element_type=F32)
    grad, vectors = call(
        dx_kernel,
        (shard_b, sds((8, width), F32)),
        (*parts, x_own, dmid, gain, dtaps, dscal, g_small),
    )
    shape = sds((blocks.shape[0] + 32, 2 * KD + VD), BF)
    slots = [pltpu.VMEM((NZ, *shape.shape), BF)]
    (message,) = call(grad_pack_kernel, (shape,), (*ring_scatter(*sent, first=True), vectors))
    (message,) = call(
        grad_join_kernel, (shape,), (place, *ring_all(message, False)), scalars=1, scratch=slots
    )
    grad_rows = gather_chips(grad)
    message, grad_rows = lax.optimization_barrier((message, grad_rows))
    received = ring_all(message, True)
    wide = tuple(a.astype(F32) for a in summed)
    received, wide = lax.optimization_barrier((received, wide))
    row = sds((1, width), F32)
    (
        g_query, g_key, g_value, d_gain, d_fgain, d_ogain, d_cq, d_ck, d_cv, g_beta, g_decay, dscal,
    ) = call(
        grad_final_kernel,
        (
            sds((width, KD), F32), sds((width, KD), F32), sds((width, VD), F32), row, row,
            sds((1, VD), F32), sds((4, KD), F32), sds((4, KD), F32), sds((4, VD), F32), row, row,
            sds((1, 128), F32),
        ),
        (place, *received),
        scalars=1,
        scratch=slots,
    )
    (grad_tokens,) = call(
        assemble_kernel, (sds((count, width), F32),), (place, *grad_rows, *(swap_core(part) for part in grad_rows)), scalars=1,
    )
    g_gate, g_up, g_down, g_out, g_outgate = wide
    return (
        block_out,
        grad_tokens,
        d_gain.reshape(width),
        g_query,
        g_key,
        g_value,
        g_outgate,
        g_beta.reshape(width, 1),
        g_decay.reshape(width, 1),
        d_cq,
        d_ck,
        d_cv,
        dscal[0, 0:1],
        dscal[0, 1:2],
        d_ogain.reshape(VD),
        g_out,
        d_fgain.reshape(width),
        g_gate,
        g_up,
        g_down,
    )


def solution(mesh):
    rows, columns = P("seq", None), P(None, "head")
    in_specs = (
        (rows, P()) + (columns,) * 9 + (P("head"), P("head"), P(), P("head", None), P())
        + (columns, columns, P("head", None), rows)
    )
    out_specs = (
        (rows, rows, P()) + (columns,) * 9 + (P("head"), P("head"), P(), P("head", None), P())
        + (columns, columns, P("head", None))
    )
    return jax.shard_map(
        per_device, mesh=mesh, in_specs=in_specs, out_specs=out_specs, check_vma=False
    )
```
